32 devices in a mesh: groups: 2 (over y), tp: 4 (over z), rows: 4 (over x, core).
Axes of the slice: x: 2, y: 2, z: 4, core: 2. Of those that a mesh axis runs over, the one named last changes fastest.
Arguments:
- hidden: bfloat16 [512, 28672], P(('groups', 'tp'), 'rows'), parts along dimension 0, may hold values from -6 to 6
- down_weight: bfloat16 [28672, 8192], P('rows', 'tp'), may hold values from -0.03125 to 0.03125
- adapter_first_factors: bfloat16 [8, 28672, 64], P('tp', 'rows'), may hold values from -0.03125 to 0.03125
- adapter_second_factors: bfloat16 [8, 64, 8192], P('rows', None, 'tp'), may hold values from -0.75 to 0.75
- segment_lengths: int32 [8, 4], P('groups'), parts along dimension 0, may hold values from 1 to 32, 64 in all within a row
- segment_adapter: int32 [8, 4], P('groups'), parts along dimension 0, may hold values from 0 to 7
- adapter_slot: int32 [8], replicated, may hold values from 0 to 7, each once
Outputs:
- mixed: bfloat16 [512, 8192], P(('groups', 'rows'), 'tp'), parts along dimension 0
The draws below stay inside these ranges and needn't reach their ends.
There are 2 independent parts, one for each index of `groups`. The reference program is written for one: setup_inputs(seed, part) draws one part's arguments, and reference() takes and returns one part's arrays. A program takes and returns all parts, laid end to end along the dimension named above; an argument that names none is the same for every part. Nothing has to cross between parts.
Inputs may be any that keep to these rules, and one draw needn't show every extreme that they name: Each row of segment_lengths sums to 64 and its largest entry is 32. `adapter_slot`: names every slot once.
All inputs are finite; a program needn't handle non-finite values.
Results may differ from the reference program's by a relative error of at most 0.0065.
Values may be sent and summed in bfloat16 or wider, within the bound.
A program may use at most 128 MiB of HBM per device.

```python
import math
import jax
import jax.numpy as jnp
import numpy as np
from jax import lax

MODEL_WIDTH = 8192
HIDDEN_UNITS = 28672
ADAPTER_RANK = 64
TOK_DEV = 64
SEGS = 4
SEG_MOST = 32
TOKENS = 256
ADAPTER_TOTAL = 8
N_TP = 4


def set_ends(entries, rng, low, high):
    extent = entries.shape
    spot = [jax.random.randint(jax.random.fold_in(rng, axis), (), 0, extent[axis]) for axis in range(len(extent))]
    entries = entries.at[tuple(spot)].set(low)
    longest = extent.index(max(extent))
    spot[longest] = (spot[longest] + 1) % extent[longest]
    return entries.at[tuple(spot)].set(high)


def block_scale(key, dims, pieces, low, top_value):
    gain, own = 1.0, jax.random.fold_in(key, 6)
    for axis_at, shards_of in pieces:
        heights = jnp.exp(jax.random.uniform(jax.random.fold_in(own, axis_at), (shards_of,), jnp.float32, low / len(pieces), top_value / len(pieces)))
        gain = gain * jnp.repeat(heights, dims[axis_at] // shards_of).reshape([-1 if axis == axis_at else 1 for axis in range(len(dims))])
    return gain


def profile(number_of, total, bound, slope):
    portions = [(1 << 20) // math.isqrt(rank ** slope) + 1 for rank in range(2, number_of + 1)]
    rest, given = total - bound - (number_of - 1), [1] * (number_of - 1)
    while rest > 0:
        free = [i for i in range(number_of - 1) if given[i] < bound]
        pool, left = sum([portions[i] for i in free]), rest
        for i in free:
            extra = min(bound - given[i], max(1, left * portions[i] // pool), rest)
            given[i] = given[i] + extra
            rest = rest - extra
    return np.array([bound] + given)


def uneven_parts(stream_key, count, total, reach, slope):
    if count == 2:
        one = jax.random.randint(stream_key, (), max(1, total - reach), min(reach, total - 1) + 1)
        return jnp.stack([one, total - one])
    sizes = jnp.asarray(profile(count, total, reach, slope), jnp.int32)
    pairs = (count - 1) // 2
    giver, taker = sizes[1:1 + 2 * pairs:2], sizes[2:2 + 2 * pairs:2]
    margin = jnp.minimum(giver - 1, reach - taker)
    passed = jax.random.randint(jax.random.fold_in(stream_key, 1), (pairs,), 0, 1 << 20) % (margin + 1)
    sizes = sizes.at[1:1 + 2 * pairs:2].set(giver - passed).at[2:2 + 2 * pairs:2].set(taker + passed)
    return sizes[jax.random.permutation(jax.random.fold_in(stream_key, 2), count)]


def scatter_about(stream_key, shape, spread, bound, shards=(), kind=jnp.bfloat16):
    array = jax.random.normal(stream_key, shape, jnp.float32) * spread
    if len(shards) > 0:
        array = block_scale(stream_key, shape, shards, -0.22, 0.18) * array
    return jnp.clip(array, min=-bound, max=bound).astype(kind)


def setup_inputs(seed: int = 0, part: int = 0) -> dict:
    keys = jax.random.split(jax.random.key(seed), 8)
    part_keys = jax.random.split(jax.random.fold_in(keys[7], part), 8)
    return {
        "hidden": scatter_about(part_keys[0], (TOKENS, HIDDEN_UNITS), 1.0, 6.0, ((0, 4), (1, 4))),
        "down_weight": scatter_about(keys[1], (HIDDEN_UNITS, MODEL_WIDTH), HIDDEN_UNITS ** -0.5, 0.03125, ((0, 4), (1, 4))),
        "adapter_first_factors": scatter_about(keys[2], (ADAPTER_TOTAL, HIDDEN_UNITS, ADAPTER_RANK), HIDDEN_UNITS ** -0.5, 0.03125, ((0, 4), (1, 4))),
        "adapter_second_factors": scatter_about(keys[3], (ADAPTER_TOTAL, ADAPTER_RANK, MODEL_WIDTH), ADAPTER_RANK ** -0.5, 0.75, ((0, 4), (2, 4))),
        "segment_lengths": jax.vmap(lambda own: uneven_parts(own, SEGS, TOK_DEV, SEG_MOST, 2))(jax.random.split(part_keys[4], N_TP)).reshape((N_TP, SEGS)).astype(jnp.int32),
        "segment_adapter": set_ends(jax.random.randint(part_keys[5], (N_TP, SEGS), 0, ADAPTER_TOTAL), jax.random.fold_in(part_keys[5], 1), 0, ADAPTER_TOTAL - 1).astype(jnp.int32),
        "adapter_slot": jax.random.permutation(keys[6], ADAPTER_TOTAL).astype(jnp.int32),
    }


def segment_table(segment_lengths, rows_each):
    ends = jnp.cumsum(segment_lengths, axis=1)
    position = lax.broadcasted_iota(jnp.int32, (1, rows_each, 1), 1)
    return jnp.sum((position >= ends[:, None, :]).astype(jnp.int32), axis=2)


def reference(hidden, down_weight, adapter_first_factors, adapter_second_factors, segment_lengths, segment_adapter, adapter_slot):
    base = jnp.dot(hidden, down_weight, preferred_element_type=jnp.float32)
    segment = segment_table(segment_lengths, TOK_DEV)
    blocks = []
    for owner_row in range(N_TP):
        prompt_block = hidden[owner_row * TOK_DEV:(owner_row + 1) * TOK_DEV]
        low_sum = jnp.zeros((TOK_DEV, MODEL_WIDTH), jnp.float32)
        for index in range(SEGS):
            storage_slot = adapter_slot[segment_adapter[owner_row, index]]
            inside = (segment[owner_row] == index)[:, None]
            shrink_step = jnp.dot(prompt_block, adapter_first_factors[storage_slot], preferred_element_type=jnp.float32)
            shrink_step = jnp.where(inside, shrink_step, jnp.zeros_like(shrink_step))
            expand_step = jnp.dot(shrink_step, adapter_second_factors[storage_slot].astype(jnp.float32), precision=lax.Precision.HIGHEST)
            low_sum = low_sum + expand_step
        blocks.append(low_sum)
    low_rank = jnp.concatenate(blocks, axis=0)
    return (base + low_rank).astype(jnp.bfloat16)
```

```python
import functools

import jax
import jax.numpy as jnp
from jax import lax
from jax.experimental import pallas as pl
from jax.experimental.pallas import tpu as pltpu
from jax.sharding import PartitionSpec as P


def slot_table(segment_lengths, segment_adapter, adapter_slot, rows_each):
    ends = jnp.cumsum(segment_lengths, axis=1)
    position = lax.broadcasted_iota(jnp.int32, (1, rows_each, 1), 1)
    segment = jnp.sum((position >= ends[:, None, :]).astype(jnp.int32), axis=2)
    seg_count = segment_lengths.shape[1]
    picks = segment[:, :, None] == lax.broadcasted_iota(jnp.int32, (1, 1, seg_count), 2)
    adapter = jnp.sum(picks.astype(jnp.int32) * segment_adapter[:, None, :], axis=2).reshape(-1)
    adapter_count = adapter_slot.shape[0]
    hits = adapter[:, None] == lax.broadcasted_iota(jnp.int32, (1, adapter_count), 1)
    return jnp.sum(hits.astype(jnp.int32) * adapter_slot[None, :], axis=1)


def reduce_shrink(partial_low):
    return lax.psum(partial_low, ("tp", "rows"))


def local(
    hidden,
    down_weight,
    adapter_first_factors,
    adapter_second_factors,
    segment_lengths,
    segment_adapter,
    adapter_slot,
):
    rows_each = hidden.shape[0]
    row_slot = slot_table(segment_lengths, segment_adapter, adapter_slot, rows_each)
    total_rows = row_slot.shape[0]
    first_factor_count = adapter_first_factors.shape[0]
    second_factor_count = adapter_second_factors.shape[0]
    rank_columns = adapter_first_factors.shape[2]
    a_first = lax.axis_index("tp") * first_factor_count
    b_first = lax.axis_index("rows") * second_factor_count
    a_pick = (
        row_slot[:, None] == a_first + lax.broadcasted_iota(jnp.int32, (1, first_factor_count), 1)
    ).astype(jnp.float32)
    b_pick = (
        row_slot[:, None] == b_first + lax.broadcasted_iota(jnp.int32, (1, second_factor_count), 1)
    ).astype(jnp.float32)
    segment_piece = lax.all_gather(hidden, "tp", axis=0, tiled=True)
    part = jnp.dot(segment_piece, down_weight, preferred_element_type=jnp.float32)
    adapter_product = jnp.einsum(
        "dm,jmh->djh", segment_piece, adapter_first_factors, preferred_element_type=jnp.float32
    )
    low_acc = jnp.sum(adapter_product * a_pick[:, :, None], axis=1)
    low_full = reduce_shrink(low_acc)
    spread = (b_pick[:, :, None] * low_full[:, None, :]).reshape(
        total_rows, second_factor_count * rank_columns
    )
    upper = spread.astype(jnp.bfloat16)
    lower = (spread - upper.astype(jnp.float32)).astype(jnp.bfloat16)
    factor_pairs = adapter_second_factors.reshape(
        second_factor_count * rank_columns, adapter_second_factors.shape[2]
    )
    low_rank = jnp.dot(upper, factor_pairs, preferred_element_type=jnp.float32) + jnp.dot(
        lower, factor_pairs, preferred_element_type=jnp.float32
    )
    prompt_block = lax.psum_scatter(part + low_rank, "rows", scatter_dimension=0, tiled=True)
    return prompt_block.astype(jnp.bfloat16)


CHUNKS = 4
TILE = 512
MESH = pl.DeviceIdType.MESH


def fused_kernel(
    hid, w, a, b, seg_len, seg_ad, slot_of, out,
    gath, wv, av, bv, acc, sh, stage, rbuf, shsel, shbuf, zsrc, zbuf,
    own_sem, w_sem, a_sem, bown_sem, b_send, b_recv,
    right_send, right_recv, left_send, left_recv,
    base_send, base_recv, sh_send, sh_recv, z_send, z_recv,
):
    t, r = lax.axis_index("tp"), lax.axis_index("rows")
    tp, chunks, rows_each, kc = gath.shape
    nrows = rbuf.shape[0]
    slots_each = av.shape[1]
    rank = av.shape[3]
    width = wv.shape[2]
    tiles = width // TILE
    up, down = lax.rem(t + 1, tp), lax.rem(t + tp - 1, tp)

    def own_copy(c):
        return pltpu.make_async_copy(
            hid.at[:, pl.ds(pl.multiple_of(c * kc, kc), kc)], gath.at[t, c], own_sem.at[c]
        )

    def w_copy(c):
        return pltpu.make_async_copy(
            w.at[pl.ds(pl.multiple_of(c * kc, kc), kc), :], wv.at[c], w_sem.at[c]
        )

    def a_copy(c):
        return pltpu.make_async_copy(
            a.at[:, pl.ds(pl.multiple_of(c * kc, kc), kc), :], av.at[c], a_sem.at[c]
        )

    def b_own():
        return pltpu.make_async_copy(b, bv.at[r], bown_sem)

    def b_copy(d):
        return pltpu.make_async_remote_copy(
            src_ref=b, dst_ref=bv.at[r], send_sem=b_send.at[d - 1], recv_sem=b_recv.at[d - 1],
            device_id={"rows": lax.rem(r + d, nrows)}, device_id_type=MESH,
        )

    def right(s, shard, c):
        return pltpu.make_async_remote_copy(
            src_ref=gath.at[shard, c], dst_ref=gath.at[shard, c],
            send_sem=right_send.at[s, c], recv_sem=right_recv.at[s, c],
            device_id={"tp": up}, device_id_type=MESH,
        )

    def left(s, shard, c):
        return pltpu.make_async_remote_copy(
            src_ref=gath.at[shard, c], dst_ref=gath.at[shard, c],
            send_sem=left_send.at[s, c], recv_sem=left_recv.at[s, c],
            device_id={"tp": down}, device_id_type=MESH,
        )

    def base_copy(j, slot, sem):
        return pltpu.make_async_remote_copy(
            src_ref=stage.at[j], dst_ref=rbuf.at[slot],
            send_sem=base_send.at[j], recv_sem=base_recv.at[sem],
            device_id={"rows": j}, device_id_type=MESH,
        )

    def sh_copy(j, slot, sem):
        return pltpu.make_async_remote_copy(
            src_ref=shsel.at[j], dst_ref=shbuf.at[slot],
            send_sem=sh_send.at[j], recv_sem=sh_recv.at[sem],
            device_id={"rows": j}, device_id_type=MESH,
        )

    def z_copy(d, slot):
        return pltpu.make_async_remote_copy(
            src_ref=zsrc, dst_ref=zbuf.at[slot],
            send_sem=z_send.at[d - 1], recv_sem=z_recv.at[d - 1],
            device_id={"tp": lax.rem(t + d, tp)}, device_id_type=MESH,
        )

    for c in range(chunks):
        own_copy(c).start()
    for c in range(chunks):
        w_copy(c).start()
        a_copy(c).start()
    b_own().start()

    barrier = pltpu.get_barrier_semaphore()
    for d in range(1, tp):
        pl.semaphore_signal(
            barrier, inc=1, device_id={"tp": lax.rem(t + d, tp)}, device_id_type=MESH
        )
    for d in range(1, nrows):
        pl.semaphore_signal(
            barrier, inc=1, device_id={"rows": lax.rem(r + d, nrows)}, device_id_type=MESH
        )
    acc[...] = jnp.zeros_like(acc)
    sh[...] = jnp.zeros_like(sh)
    pl.semaphore_wait(barrier, tp - 1 + nrows - 1)

    for c in range(chunks):
        own_copy(c).wait()

        @pl.when(t < tp - 1)
        def _():
            right(0, t, c).start()

        @pl.when(t > 0)
        def _():
            left(0, t, c).start()

    for d in range(1, nrows):
        b_copy(d).start()

    def slots_in(j):
        position = lax.broadcasted_iota(jnp.int32, (rows_each, rank), 0)
        slot = jnp.zeros((rows_each, rank), jnp.int32)
        end = jnp.int32(0)
        for k in range(seg_len.shape[1]):
            slot = jnp.where(position >= end, slot_of[seg_ad[j, k]], slot)
            end = end + seg_len[j, k]
        return slot

    def compute(shard, c):
        for q in range(slots_each):
            sh[shard, q] += jnp.dot(
                gath[shard, c], av[c, q], preferred_element_type=jnp.float32
            )

        def tile_step(n, carry):
            cols = pl.ds(pl.multiple_of(n * TILE, TILE), TILE)
            acc[shard, :, cols] += jnp.dot(
                gath[shard, c], wv[c, :, cols], preferred_element_type=jnp.float32
            )
            return carry

        lax.fori_loop(0, tiles, tile_step, 0)

    def finish(j):
        slot = slots_in(j)
        picked = jnp.zeros((rows_each, rank), jnp.float32)
        for q in range(slots_each):
            picked += jnp.where(slot == t * slots_each + q, sh[j, q], 0.0)
        shsel[j] = picked

        @pl.when(j != r)
        def _():
            sh_copy(j, r, r).start()
            stage[j] = acc[j].astype(jnp.bfloat16)
            base_copy(j, r, r).start()

    def own_step(c, carry):
        w_copy(c).wait()
        a_copy(c).wait()
        compute(t, c)
        return carry

    lax.fori_loop(0, chunks, own_step, 0)
    finish(t)

    def ring_step(i, carry):
        s, c = i // chunks, i % chunks
        low, high = t - 1 - s, t + 1 + s

        @pl.when(low >= 0)
        def _():
            right(s, low, c).wait_recv()

            @pl.when(t < tp - 1)
            def _():
                right(s + 1, low, c).start()

            compute(low, c)

            @pl.when(c == chunks - 1)
            def _():
                finish(low)

        @pl.when(high <= tp - 1)
        def _():
            left(s, high, c).wait_recv()

            @pl.when(t > 0)
            def _():
                left(s + 1, high, c).start()

            compute(high, c)

            @pl.when(c == chunks - 1)
            def _():
                finish(high)

        return carry

    lax.fori_loop(0, (tp - 1) * chunks, ring_step, 0)

    total = shsel[r]
    for d in range(1, nrows):
        other = lax.rem(r + d, nrows)
        sh_copy(other, other, other).wait_recv()
        total = total + shbuf[other]
    zsrc[...] = total
    for d in range(1, tp):
        z_copy(d, t).start()
    b_own().wait()
    for d in range(1, nrows):
        b_copy(d).wait_recv()
    slot = slots_in(r)
    for d in range(1, tp):
        source = lax.rem(t + tp - d, tp)
        z_copy(d, source).wait_recv()
        total = total + zbuf[source]
    spread = jnp.concatenate(
        [jnp.where(slot == q, total, 0.0) for q in range(slot_of.shape[0])], axis=1
    )
    upper = spread.astype(jnp.bfloat16)
    lower = (spread - upper.astype(jnp.float32)).astype(jnp.bfloat16)
    pair = jnp.concatenate([upper, lower], axis=0)
    for d in range(1, nrows):
        other = lax.rem(r + d, nrows)
        base_copy(other, other, other).wait_recv()
    depth = bv.shape[0] * bv.shape[1]
    for n in range(tiles):
        cols = slice(n * TILE, (n + 1) * TILE)
        both = jnp.dot(
            pair, bv[:, :, cols].reshape(depth, TILE), preferred_element_type=jnp.float32
        )
        value = both[:rows_each] + both[rows_each:] + acc[r, :, cols]
        for d in range(1, nrows):
            other = lax.rem(r + d, nrows)
            value += rbuf[other, :, cols].astype(jnp.float32)
        out[:, cols] = value.astype(out.dtype)

    def drain(i, carry):
        s, c = i // chunks, i % chunks

        @pl.when((t < tp - 1) & (t - s >= 0))
        def _():
            right(s, t - s, c).wait_send()

        @pl.when((t > 0) & (t + s <= tp - 1))
        def _():
            left(s, t + s, c).wait_send()

        return carry

    lax.fori_loop(0, (tp - 1) * chunks, drain, 0)
    for d in range(1, nrows):
        other = lax.rem(r + d, nrows)
        b_copy(d).wait_send()
        sh_copy(other, r, r).wait_send()
        base_copy(other, r, r).wait_send()
    for d in range(1, tp):
        z_copy(d, t).wait_send()


def fused(tp, nrows, hidden, down_weight, first, second, seg_len, seg_ad, slot_of):
    rows_each, depth = hidden.shape
    width = down_weight.shape[1]
    kc = depth // CHUNKS
    slots_each, _, rank = first.shape
    owned = second.shape[0] * second.shape[1]
    second = second.reshape(owned, width)
    dma = pltpu.SemaphoreType.DMA
    anywhere = pl.BlockSpec(memory_space=pl.ANY)
    scalars = pl.BlockSpec(memory_space=pltpu.SMEM)
    return pl.pallas_call(
        fused_kernel,
        out_shape=jax.ShapeDtypeStruct((rows_each, width), jnp.bfloat16),
        in_specs=[anywhere] * 4 + [scalars] * 3,
        out_specs=pl.BlockSpec(memory_space=pltpu.VMEM),
        scratch_shapes=[
            pltpu.VMEM((tp, CHUNKS, rows_each, kc), jnp.bfloat16),
            pltpu.VMEM((CHUNKS, kc, width), jnp.bfloat16),
            pltpu.VMEM((CHUNKS, slots_each, kc, rank), jnp.bfloat16),
            pltpu.VMEM((nrows, owned, width), jnp.bfloat16),
            pltpu.VMEM((tp, rows_each, width), jnp.float32),
            pltpu.VMEM((tp, slots_each, rows_each, rank), jnp.float32),
            pltpu.VMEM((tp, rows_each, width), jnp.bfloat16),
            pltpu.VMEM((nrows, rows_each, width), jnp.bfloat16),
            pltpu.VMEM((tp, rows_each, rank), jnp.float32),
            pltpu.VMEM((nrows, rows_each, rank), jnp.float32),
            pltpu.VMEM((rows_each, rank), jnp.float32),
            pltpu.VMEM((tp, rows_each, rank), jnp.float32),
            dma((CHUNKS,)), dma((CHUNKS,)), dma((CHUNKS,)), dma,
            dma((nrows - 1,)), dma((nrows - 1,)),
            dma((tp - 1, CHUNKS)), dma((tp - 1, CHUNKS)),
            dma((tp - 1, CHUNKS)), dma((tp - 1, CHUNKS)),
            dma((tp,)), dma((nrows,)), dma((tp,)), dma((nrows,)),
            dma((tp - 1,)), dma((tp - 1,)),
        ],
        compiler_params=pltpu.CompilerParams(
            collective_id=0, has_side_effects=True, vmem_limit_bytes=56 * 2**20
        ),
        cost_estimate=pl.CostEstimate(
            flops=2 * tp * rows_each * depth * width,
            bytes_accessed=2 * depth * width,
            transcendentals=0,
        ),
    )(hidden, down_weight, first, second, seg_len, seg_ad, slot_of)


def solution(mesh):
    placed = (
        P(("groups", "tp"), "rows"),
        P("rows", "tp"),
        P("tp", "rows", None),
        P("rows", None, "tp"),
        P("groups", None),
        P("groups", None),
        P(),
    )
    tp, nrows = mesh.shape["tp"], mesh.shape["rows"]
    body = functools.partial(fused, tp, nrows) if tp == nrows and tp <= 4 else local
    return jax.shard_map(
        body, mesh=mesh, in_specs=placed, out_specs=P(("groups", "rows"), "tp"), check_vma=False
    )
```

```python
import functools

import jax
import jax.numpy as jnp
from jax import lax
from jax.experimental import pallas as pl
from jax.experimental.pallas import tpu as pltpu
from jax.sharding import PartitionSpec as P


def slot_table(segment_lengths, segment_adapter, adapter_slot, rows_each):
    ends = jnp.cumsum(segment_lengths, axis=1)
    position = lax.broadcasted_iota(jnp.int32, (1, rows_each, 1), 1)
    segment = jnp.sum((position >= ends[:, None, :]).astype(jnp.int32), axis=2)
    seg_count = segment_lengths.shape[1]
    picks = segment[:, :, None] == lax.broadcasted_iota(jnp.int32, (1, 1, seg_count), 2)
    adapter = jnp.sum(picks.astype(jnp.int32) * segment_adapter[:, None, :], axis=2).reshape(-1)
    adapter_count = adapter_slot.shape[0]
    hits = adapter[:, None] == lax.broadcasted_iota(jnp.int32, (1, adapter_count), 1)
    return jnp.sum(hits.astype(jnp.int32) * adapter_slot[None, :], axis=1)


def reduce_shrink(partial_low):
    return lax.psum(partial_low, ("tp", "rows"))


def local(
    hidden,
    down_weight,
    adapter_first_factors,
    adapter_second_factors,
    segment_lengths,
    segment_adapter,
    adapter_slot,
):
    rows_each = hidden.shape[0]
    row_slot = slot_table(segment_lengths, segment_adapter, adapter_slot, rows_each)
    total_rows = row_slot.shape[0]
    first_factor_count = adapter_first_factors.shape[0]
    second_factor_count = adapter_second_factors.shape[0]
    rank_columns = adapter_first_factors.shape[2]
    a_first = lax.axis_index("tp") * first_factor_count
    b_first = lax.axis_index("rows") * second_factor_count
    a_pick = (
        row_slot[:, None] == a_first + lax.broadcasted_iota(jnp.int32, (1, first_factor_count), 1)
    ).astype(jnp.float32)
    b_pick = (
        row_slot[:, None] == b_first + lax.broadcasted_iota(jnp.int32, (1, second_factor_count), 1)
    ).astype(jnp.float32)
    segment_piece = lax.all_gather(hidden, "tp", axis=0, tiled=True)
    part = jnp.dot(segment_piece, down_weight, preferred_element_type=jnp.float32)
    adapter_product = jnp.einsum(
        "dm,jmh->djh", segment_piece, adapter_first_factors, preferred_element_type=jnp.float32
    )
    low_acc = jnp.sum(adapter_product * a_pick[:, :, None], axis=1)
    low_full = reduce_shrink(low_acc)
    spread = (b_pick[:, :, None] * low_full[:, None, :]).reshape(
        total_rows, second_factor_count * rank_columns
    )
    upper = spread.astype(jnp.bfloat16)
    lower = (spread - upper.astype(jnp.float32)).astype(jnp.bfloat16)
    factor_pairs = adapter_second_factors.reshape(
        second_factor_count * rank_columns, adapter_second_factors.shape[2]
    )
    low_rank = jnp.dot(upper, factor_pairs, preferred_element_type=jnp.float32) + jnp.dot(
        lower, factor_pairs, preferred_element_type=jnp.float32
    )
    prompt_block = lax.psum_scatter(part + low_rank, "rows", scatter_dimension=0, tiled=True)
    return prompt_block.astype(jnp.bfloat16)


CHUNKS = 4
TILE = 512
MESH = pl.DeviceIdType.MESH


def fused_kernel(
    hid, w, a, b, seg_len, seg_ad, slot_of, out,
    gath, wv, av, bv, acc, sh, stage, rbuf, shsel, shbuf, zsrc, zbuf,
    own_sem, w_sem, a_sem, bown_sem, b_send, b_recv,
    right_send, right_recv, left_send, left_recv,
    base_send, base_recv, sh_send, sh_recv, z_send, z_recv,
):
    t, r = lax.axis_index("tp"), lax.axis_index("rows")
    tp, chunks, rows_each, kc = gath.shape
    nrows = rbuf.shape[0]
    slots_each = av.shape[1]
    rank = av.shape[2]
    width = wv.shape[2]
    tiles = width // TILE
    up, down = lax.rem(t + 1, tp), lax.rem(t + tp - 1, tp)

    def own_copy(c):
        return pltpu.make_async_copy(
            hid.at[:, pl.ds(pl.multiple_of(c * kc, kc), kc)], gath.at[t, c], own_sem.at[c]
        )

    def w_copy(c):
        return pltpu.make_async_copy(
            w.at[pl.ds(pl.multiple_of(c * kc, kc), kc), :], wv.at[c], w_sem.at[c]
        )

    def a_copy(c):
        return pltpu.make_async_copy(
            a.at[:, :, pl.ds(pl.multiple_of(c * kc, kc), kc)], av.at[c], a_sem.at[c]
        )

    def b_own():
        return pltpu.make_async_copy(b, bv.at[r], bown_sem)

    def b_copy(d):
        return pltpu.make_async_remote_copy(
            src_ref=b, dst_ref=bv.at[r], send_sem=b_send.at[d - 1], recv_sem=b_recv.at[d - 1],
            device_id={"rows": lax.rem(r + d, nrows)}, device_id_type=MESH,
        )

    def right(s, shard, c):
        return pltpu.make_async_remote_copy(
            src_ref=gath.at[shard, c], dst_ref=gath.at[shard, c],
            send_sem=right_send.at[s, c], recv_sem=right_recv.at[s, c],
            device_id={"tp": up}, device_id_type=MESH,
        )

    def left(s, shard, c):
        return pltpu.make_async_remote_copy(
            src_ref=gath.at[shard, c], dst_ref=gath.at[shard, c],
            send_sem=left_send.at[s, c], recv_sem=left_recv.at[s, c],
            device_id={"tp": down}, device_id_type=MESH,
        )

    def base_copy(j, n, slot):
        return pltpu.make_async_remote_copy(
            src_ref=stage.at[j, n], dst_ref=rbuf.at[slot, n],
            send_sem=base_send.at[j, n], recv_sem=base_recv.at[slot, n],
            device_id={"rows": j}, device_id_type=MESH,
        )

    def sh_copy(j, slot, sem):
        return pltpu.make_async_remote_copy(
            src_ref=shsel.at[j], dst_ref=shbuf.at[slot],
            send_sem=sh_send.at[j], recv_sem=sh_recv.at[sem],
            device_id={"rows": j}, device_id_type=MESH,
        )

    def z_copy(d, slot):
        return pltpu.make_async_remote_copy(
            src_ref=zsrc, dst_ref=zbuf.at[slot],
            send_sem=z_send.at[d - 1], recv_sem=z_recv.at[d - 1],
            device_id={"tp": lax.rem(t + d, tp)}, device_id_type=MESH,
        )

    for c in range(chunks):
        own_copy(c).start()

    barrier = pltpu.get_barrier_semaphore()
    for d in range(1, tp):
        pl.semaphore_signal(
            barrier, inc=1, device_id={"tp": lax.rem(t + d, tp)}, device_id_type=MESH
        )
    for d in range(1, nrows):
        pl.semaphore_signal(
            barrier, inc=1, device_id={"rows": lax.rem(r + d, nrows)}, device_id_type=MESH
        )
    acc[...] = jnp.zeros_like(acc)
    sh[...] = jnp.zeros_like(sh)
    pl.semaphore_wait(barrier, tp - 1 + nrows - 1)

    for c in range(chunks):
        own_copy(c).wait()

        @pl.when(t < tp - 1)
        def _():
            right(0, t, c).start()

        @pl.when(t > 0)
        def _():
            left(0, t, c).start()

    for c in range(chunks):
        w_copy(c).start()
        a_copy(c).start()
    b_own().start()
    for d in range(1, nrows):
        b_copy(d).start()

    def slots_in(j):
        position = lax.broadcasted_iota(jnp.int32, (rows_each, rank), 0)
        slot = jnp.zeros((rows_each, rank), jnp.int32)
        end = jnp.int32(0)
        for k in range(seg_len.shape[1]):
            slot = jnp.where(position >= end, slot_of[seg_ad[j, k]], slot)
            end = end + seg_len[j, k]
        return slot

    def compute(shard, c):
        last = c == chunks - 1
        piece = gath[shard, c]
        sh[shard] += lax.dot_general(
            piece, av[c].reshape(slots_each * rank, kc), (((1,), (1,)), ((), ())),
            preferred_element_type=jnp.float32,
        )

        @pl.when(last)
        def _():
            send_shrink(shard)

        def tile_step(n, carry):
            cols = pl.ds(pl.multiple_of(n * TILE, TILE), TILE)
            acc[shard, n] += jnp.dot(
                gath[shard, c], wv[c, :, cols], preferred_element_type=jnp.float32
            )

            @pl.when(last & (shard != r))
            def _():
                stage[shard, n] = acc[shard, n].astype(jnp.bfloat16)
                base_copy(shard, n, r).start()

            return carry

        lax.fori_loop(0, tiles, tile_step, 0)

    def send_shrink(j):
        slot = slots_in(j)
        picked = jnp.zeros((rows_each, rank), jnp.float32)
        for q in range(slots_each):
            picked += jnp.where(
                slot == t * slots_each + q, sh[j, :, q * rank:(q + 1) * rank], 0.0
            )
        shsel[j] = picked

        @pl.when(j != r)
        def _():
            sh_copy(j, r, r).start()

    def own_step(c, carry):
        w_copy(c).wait()
        a_copy(c).wait()
        compute(t, c)
        return carry

    lax.fori_loop(0, chunks, own_step, 0)

    def ring_step(i, carry):
        s, c = i // chunks, i % chunks
        low, high = t - 1 - s, t + 1 + s

        @pl.when(low >= 0)
        def _():
            right(s, low, c).wait_recv()

            @pl.when(t < tp - 1)
            def _():
                right(s + 1, low, c).start()

            compute(low, c)

        @pl.when(high <= tp - 1)
        def _():
            left(s, high, c).wait_recv()

            @pl.when(t > 0)
            def _():
                left(s + 1, high, c).start()

            compute(high, c)

        return carry

    lax.fori_loop(0, (tp - 1) * chunks, ring_step, 0)

    total = shsel[r]
    for d in range(1, nrows):
        other = lax.rem(r + d, nrows)
        sh_copy(other, other, other).wait_recv()
        total = total + shbuf[other]
    zsrc[...] = total
    for d in range(1, tp):
        z_copy(d, t).start()
    b_own().wait()
    for d in range(1, nrows):
        b_copy(d).wait_recv()
    slot = slots_in(r)
    for d in range(1, tp):
        source = lax.rem(t + tp - d, tp)
        z_copy(d, source).wait_recv()
        total = total + zbuf[source]
    spread = jnp.concatenate(
        [jnp.where(slot == q, total, 0.0) for q in range(slot_of.shape[0])], axis=1
    )
    upper = spread.astype(jnp.bfloat16)
    lower = (spread - upper.astype(jnp.float32)).astype(jnp.bfloat16)
    pair = jnp.concatenate([upper, lower], axis=0)
    depth = bv.shape[0] * bv.shape[1]
    for n in range(tiles):
        both = jnp.dot(
            pair, bv[:, :, n * TILE:(n + 1) * TILE].reshape(depth, TILE),
            preferred_element_type=jnp.float32,
        )
        acc[r, n] += both[:rows_each] + both[rows_each:]
    for n in range(tiles):
        value = acc[r, n]
        for d in range(1, nrows):
            other = lax.rem(r + d, nrows)
            base_copy(other, n, other).wait_recv()
            value += rbuf[other, n].astype(jnp.float32)
        out[:, n * TILE:(n + 1) * TILE] = value.astype(out.dtype)

    def drain(i, carry):
        s, c = i // chunks, i % chunks

        @pl.when((t < tp - 1) & (t - s >= 0))
        def _():
            right(s, t - s, c).wait_send()

        @pl.when((t > 0) & (t + s <= tp - 1))
        def _():
            left(s, t + s, c).wait_send()

        return carry

    lax.fori_loop(0, (tp - 1) * chunks, drain, 0)
    for d in range(1, nrows):
        other = lax.rem(r + d, nrows)
        b_copy(d).wait_send()
        sh_copy(other, r, r).wait_send()
        for n in range(tiles):
            base_copy(other, n, r).wait_send()
    for d in range(1, tp):
        z_copy(d, t).wait_send()


def fused(tp, nrows, hidden, down_weight, first, second, seg_len, seg_ad, slot_of):
    rows_each, depth = hidden.shape
    width = down_weight.shape[1]
    kc = depth // CHUNKS
    slots_each, _, rank = first.shape
    first = first.transpose(0, 2, 1)
    owned = second.shape[0] * second.shape[1]
    second = second.reshape(owned, width)
    dma = pltpu.SemaphoreType.DMA
    anywhere = pl.BlockSpec(memory_space=pl.ANY)
    scalars = pl.BlockSpec(memory_space=pltpu.SMEM)
    return pl.pallas_call(
        fused_kernel,
        out_shape=jax.ShapeDtypeStruct((rows_each, width), jnp.bfloat16),
        in_specs=[anywhere] * 4 + [scalars] * 3,
        out_specs=pl.BlockSpec(memory_space=pltpu.VMEM),
        scratch_shapes=[
            pltpu.VMEM((tp, CHUNKS, rows_each, kc), jnp.bfloat16),
            pltpu.VMEM((CHUNKS, kc, width), jnp.bfloat16),
            pltpu.VMEM((CHUNKS, slots_each, rank, kc), jnp.bfloat16),
            pltpu.VMEM((nrows, owned, width), jnp.bfloat16),
            pltpu.VMEM((tp, width // TILE, rows_each, TILE), jnp.float32),
            pltpu.VMEM((tp, rows_each, slots_each * rank), jnp.float32),
            pltpu.VMEM((tp, width // TILE, rows_each, TILE), jnp.bfloat16),
            pltpu.VMEM((nrows, width // TILE, rows_each, TILE), jnp.bfloat16),
            pltpu.VMEM((tp, rows_each, rank), jnp.float32),
            pltpu.VMEM((nrows, rows_each, rank), jnp.float32),
            pltpu.VMEM((rows_each, rank), jnp.float32),
            pltpu.VMEM((tp, rows_each, rank), jnp.float32),
            dma((CHUNKS,)), dma((CHUNKS,)), dma((CHUNKS,)), dma,
            dma((nrows - 1,)), dma((nrows - 1,)),
            dma((tp - 1, CHUNKS)), dma((tp - 1, CHUNKS)),
            dma((tp - 1, CHUNKS)), dma((tp - 1, CHUNKS)),
            dma((tp, width // TILE)), dma((nrows, width // TILE)), dma((tp,)), dma((nrows,)),
            dma((tp - 1,)), dma((tp - 1,)),
        ],
        compiler_params=pltpu.CompilerParams(
            collective_id=0, has_side_effects=True, vmem_limit_bytes=56 * 2**20
        ),
        cost_estimate=pl.CostEstimate(
            flops=2 * tp * rows_each * depth * width,
            bytes_accessed=2 * depth * width,
            transcendentals=0,
        ),
    )(hidden, down_weight, first, second, seg_len, seg_ad, slot_of)


def solution(mesh):
    placed = (
        P(("groups", "tp"), "rows"),
        P("rows", "tp"),
        P("tp", "rows", None),
        P("rows", None, "tp"),
        P("groups", None),
        P("groups", None),
        P(),
    )
    tp, nrows = mesh.shape["tp"], mesh.shape["rows"]
    body = functools.partial(fused, tp, nrows) if tp == nrows and tp <= 4 else local
    return jax.shard_map(
        body, mesh=mesh, in_specs=placed, out_specs=P(("groups", "rows"), "tp"), check_vma=False
    )
```

```python
import functools

import jax
import jax.numpy as jnp
from jax import lax
from jax.experimental import pallas as pl
from jax.experimental.pallas import tpu as pltpu
from jax.sharding import PartitionSpec as P


def slot_table(segment_lengths, segment_adapter, adapter_slot, rows_each):
    ends = jnp.cumsum(segment_lengths, axis=1)
    position = lax.broadcasted_iota(jnp.int32, (1, rows_each, 1), 1)
    segment = jnp.sum((position >= ends[:, None, :]).astype(jnp.int32), axis=2)
    seg_count = segment_lengths.shape[1]
    picks = segment[:, :, None] == lax.broadcasted_iota(jnp.int32, (1, 1, seg_count), 2)
    adapter = jnp.sum(picks.astype(jnp.int32) * segment_adapter[:, None, :], axis=2).reshape(-1)
    adapter_count = adapter_slot.shape[0]
    hits = adapter[:, None] == lax.broadcasted_iota(jnp.int32, (1, adapter_count), 1)
    return jnp.sum(hits.astype(jnp.int32) * adapter_slot[None, :], axis=1)


def reduce_shrink(partial_low):
    return lax.psum(partial_low, ("tp", "rows"))


def local(
    hidden,
    down_weight,
    adapter_first_factors,
    adapter_second_factors,
    segment_lengths,
    segment_adapter,
    adapter_slot,
):
    rows_each = hidden.shape[0]
    row_slot = slot_table(segment_lengths, segment_adapter, adapter_slot, rows_each)
    total_rows = row_slot.shape[0]
    first_factor_count = adapter_first_factors.shape[0]
    second_factor_count = adapter_second_factors.shape[0]
    rank_columns = adapter_first_factors.shape[2]
    a_first = lax.axis_index("tp") * first_factor_count
    b_first = lax.axis_index("rows") * second_factor_count
    a_pick = (
        row_slot[:, None] == a_first + lax.broadcasted_iota(jnp.int32, (1, first_factor_count), 1)
    ).astype(jnp.float32)
    b_pick = (
        row_slot[:, None] == b_first + lax.broadcasted_iota(jnp.int32, (1, second_factor_count), 1)
    ).astype(jnp.float32)
    segment_piece = lax.all_gather(hidden, "tp", axis=0, tiled=True)
    part = jnp.dot(segment_piece, down_weight, preferred_element_type=jnp.float32)
    adapter_product = jnp.einsum(
        "dm,jmh->djh", segment_piece, adapter_first_factors, preferred_element_type=jnp.float32
    )
    low_acc = jnp.sum(adapter_product * a_pick[:, :, None], axis=1)
    low_full = reduce_shrink(low_acc)
    spread = (b_pick[:, :, None] * low_full[:, None, :]).reshape(
        total_rows, second_factor_count * rank_columns
    )
    upper = spread.astype(jnp.bfloat16)
    lower = (spread - upper.astype(jnp.float32)).astype(jnp.bfloat16)
    factor_pairs = adapter_second_factors.reshape(
        second_factor_count * rank_columns, adapter_second_factors.shape[2]
    )
    low_rank = jnp.dot(upper, factor_pairs, preferred_element_type=jnp.float32) + jnp.dot(
        lower, factor_pairs, preferred_element_type=jnp.float32
    )
    prompt_block = lax.psum_scatter(part + low_rank, "rows", scatter_dimension=0, tiled=True)
    return prompt_block.astype(jnp.bfloat16)


CHUNKS = 4
TILE = 512
MESH = pl.DeviceIdType.MESH


def fused_kernel(
    hid, w, a, b, seg_len, seg_ad, slot_of, out,
    gath, wv, av, bv, acc, sh, stage, rbuf, mbuf, shsel, shbuf, zsrc, zbuf,
    own_sem, w_sem, a_sem, bown_sem, b_send, b_recv,
    right_send, right_recv, left_send, left_recv,
    base_send, base_recv, mate_send, mate_recv, sh_send, sh_recv, z_send, z_recv,
):
    t, r = lax.axis_index("tp"), lax.axis_index("rows")
    tp, chunks, rows_each, kc = gath.shape
    nrows = shbuf.shape[0]
    slots_each = av.shape[1]
    rank = av.shape[2]
    width = wv.shape[2]
    tiles = width // TILE
    part = tiles // 2
    core, chip = r % 2, r // 2
    mate = r + 1 - 2 * core
    late = ((t == 0) & (r == tp - 1)) | ((t == tp - 1) & (r == 0))
    up, down = lax.rem(t + 1, tp), lax.rem(t + tp - 1, tp)

    def own_copy(c):
        return pltpu.make_async_copy(
            hid.at[:, pl.ds(pl.multiple_of(c * kc, kc), kc)], gath.at[t, c], own_sem.at[c]
        )

    def w_copy(c):
        return pltpu.make_async_copy(
            w.at[pl.ds(pl.multiple_of(c * kc, kc), kc), :], wv.at[c], w_sem.at[c]
        )

    def a_copy(c):
        return pltpu.make_async_copy(
            a.at[:, :, pl.ds(pl.multiple_of(c * kc, kc), kc)], av.at[c], a_sem.at[c]
        )

    def b_own():
        return pltpu.make_async_copy(b, bv.at[r], bown_sem)

    def b_copy(d):
        return pltpu.make_async_remote_copy(
            src_ref=b, dst_ref=bv.at[r], send_sem=b_send.at[d - 1], recv_sem=b_recv.at[d - 1],
            device_id={"rows": lax.rem(r + d, nrows)}, device_id_type=MESH,
        )

    def right(s, shard, c):
        return pltpu.make_async_remote_copy(
            src_ref=gath.at[shard, c], dst_ref=gath.at[shard, c],
            send_sem=right_send.at[s, c], recv_sem=right_recv.at[s, c],
            device_id={"tp": up}, device_id_type=MESH,
        )

    def left(s, shard, c):
        return pltpu.make_async_remote_copy(
            src_ref=gath.at[shard, c], dst_ref=gath.at[shard, c],
            send_sem=left_send.at[s, c], recv_sem=left_recv.at[s, c],
            device_id={"tp": down}, device_id_type=MESH,
        )

    def base_copy(j, n, slot):
        return pltpu.make_async_remote_copy(
            src_ref=stage.at[j, n], dst_ref=rbuf.at[slot, n],
            send_sem=base_send.at[j, n], recv_sem=base_recv.at[slot, n],
            device_id={"rows": j}, device_id_type=MESH,
        )

    def mate_copy(j, n):
        return pltpu.make_async_remote_copy(
            src_ref=stage.at[j, n], dst_ref=mbuf.at[j, n],
            send_sem=mate_send.at[j, n], recv_sem=mate_recv.at[j, n],
            device_id={"rows": mate}, device_id_type=MESH,
        )

    def sh_copy(j, slot, sem):
        return pltpu.make_async_remote_copy(
            src_ref=shsel.at[j], dst_ref=shbuf.at[slot],
            send_sem=sh_send.at[j], recv_sem=sh_recv.at[sem],
            device_id={"rows": j}, device_id_type=MESH,
        )

    def z_copy(d, slot):
        return pltpu.make_async_remote_copy(
            src_ref=zsrc, dst_ref=zbuf.at[slot],
            send_sem=z_send.at[d - 1], recv_sem=z_recv.at[d - 1],
            device_id={"tp": lax.rem(t + d, tp)}, device_id_type=MESH,
        )

    for c in range(chunks):
        own_copy(c).start()

    barrier = pltpu.get_barrier_semaphore()
    for d in range(1, tp):
        pl.semaphore_signal(
            barrier, inc=1, device_id={"tp": lax.rem(t + d, tp)}, device_id_type=MESH
        )
    for d in range(1, nrows):
        pl.semaphore_signal(
            barrier, inc=1, device_id={"rows": lax.rem(r + d, nrows)}, device_id_type=MESH
        )
    acc[...] = jnp.zeros_like(acc)
    sh[...] = jnp.zeros_like(sh)
    pl.semaphore_wait(barrier, tp - 1 + nrows - 1)

    for c in range(chunks):
        own_copy(c).wait()

        @pl.when(t < tp - 1)
        def _():
            right(0, t, c).start()

        @pl.when(t > 0)
        def _():
            left(0, t, c).start()

    for c in range(chunks):
        w_copy(c).start()
        a_copy(c).start()
    b_own().start()
    for d in range(1, nrows):
        b_copy(d).start()

    def slots_in(j):
        position = lax.broadcasted_iota(jnp.int32, (rows_each, rank), 0)
        slot = jnp.zeros((rows_each, rank), jnp.int32)
        end = jnp.int32(0)
        for k in range(seg_len.shape[1]):
            slot = jnp.where(position >= end, slot_of[seg_ad[j, k]], slot)
            end = end + seg_len[j, k]
        return slot

    def exchange_shrink():
        total = shsel[r]
        for d in range(1, nrows):
            other = lax.rem(r + d, nrows)
            sh_copy(other, other, other).wait_recv()
            total = total + shbuf[other]
        zsrc[...] = total
        for d in range(1, tp):
            z_copy(d, t).start()

    def compute(shard, c):
        last = c == chunks - 1
        piece = gath[shard, c]
        sh[shard] += lax.dot_general(
            piece, av[c].reshape(slots_each * rank, kc), (((1,), (1,)), ((), ())),
            preferred_element_type=jnp.float32,
        )

        @pl.when(last)
        def _():
            send_shrink(shard)

        def tile_step(m, carry):
            n = lax.rem(m + (1 - core) * part, tiles)
            cols = pl.ds(pl.multiple_of(n * TILE, TILE), TILE)
            @pl.when(last & (shard == r) & late & (m == 1))
            def _():
                exchange_shrink()

            acc[shard, n] += jnp.dot(
                gath[shard, c], wv[c, :, cols], preferred_element_type=jnp.float32
            )

            @pl.when(last & (shard == mate))
            def _():
                stage[shard, n] = acc[shard, n].astype(jnp.bfloat16)
                base_copy(shard, n, 0).start()

            @pl.when(last & (shard // 2 != chip) & (m < part))
            def _():
                stage[shard, n] = acc[shard, n].astype(jnp.bfloat16)
                mate_copy(shard, n).start()

            @pl.when(last & (shard // 2 != chip) & (m >= part))
            def _():
                mate_copy(shard, n).wait_recv()
                both = acc[shard, n] + mbuf[shard, n].astype(jnp.float32)
                stage[shard, n] = both.astype(jnp.bfloat16)
                base_copy(shard, n, 1).start()

            return carry

        lax.fori_loop(0, tiles, tile_step, 0)

    def send_shrink(j):
        slot = slots_in(j)
        picked = jnp.zeros((rows_each, rank), jnp.float32)
        for q in range(slots_each):
            picked += jnp.where(
                slot == t * slots_each + q, sh[j, :, q * rank:(q + 1) * rank], 0.0
            )
        shsel[j] = picked

        @pl.when(j != r)
        def _():
            sh_copy(j, r, r).start()

    def own_step(c, carry):
        w_copy(c).wait()
        a_copy(c).wait()
        compute(t, c)
        return carry

    lax.fori_loop(0, chunks, own_step, 0)

    def ring_step(i, carry):
        s, c = i // chunks, i % chunks
        low, high = t - 1 - s, t + 1 + s

        @pl.when((i == (tp - 1) * chunks - 1) & jnp.logical_not(late))
        def _():
            exchange_shrink()

        @pl.when(low >= 0)
        def _():
            right(s, low, c).wait_recv()

            @pl.when(t < tp - 1)
            def _():
                right(s + 1, low, c).start()

            compute(low, c)

        @pl.when(high <= tp - 1)
        def _():
            left(s, high, c).wait_recv()

            @pl.when(t > 0)
            def _():
                left(s + 1, high, c).start()

            compute(high, c)

        return carry

    lax.fori_loop(0, (tp - 1) * chunks, ring_step, 0)

    total = zsrc[...]
    b_own().wait()
    for d in range(1, nrows):
        b_copy(d).wait_recv()
    slot = slots_in(r)
    for d in range(1, tp):
        source = lax.rem(t + tp - d, tp)
        z_copy(d, source).wait_recv()
        total = total + zbuf[source]
    spread = jnp.concatenate(
        [jnp.where(slot == q, total, 0.0) for q in range(slot_of.shape[0])], axis=1
    )
    upper = spread.astype(jnp.bfloat16)
    lower = (spread - upper.astype(jnp.float32)).astype(jnp.bfloat16)
    pair = jnp.concatenate([upper, lower], axis=0)
    depth = bv.shape[0] * bv.shape[1]
    for n in range(tiles):
        both = jnp.dot(
            pair, bv[:, :, n * TILE:(n + 1) * TILE].reshape(depth, TILE),
            preferred_element_type=jnp.float32,
        )
        acc[r, n] += both[:rows_each] + both[rows_each:]
    for n in range(tiles):
        value = acc[r, n]
        for k in range(2):
            base_copy(mate, n, k).wait_recv()
            value += rbuf[k, n].astype(jnp.float32)
        out[:, n * TILE:(n + 1) * TILE] = value.astype(out.dtype)

    def drain(i, carry):
        s, c = i // chunks, i % chunks

        @pl.when((t < tp - 1) & (t - s >= 0))
        def _():
            right(s, t - s, c).wait_send()

        @pl.when((t > 0) & (t + s <= tp - 1))
        def _():
            left(s, t + s, c).wait_send()

        return carry

    lax.fori_loop(0, (tp - 1) * chunks, drain, 0)
    for d in range(1, nrows):
        other = lax.rem(r + d, nrows)
        b_copy(d).wait_send()
        sh_copy(other, r, r).wait_send()
    for n in range(tiles):
        base_copy(mate, n, 0).wait_send()
    for k in range(2):
        far = 2 * (1 - chip) + k
        for m in range(part):
            mate_copy(far, (1 - core) * part + m).wait_send()
            base_copy(far, core * part + m, 1).wait_send()
    for d in range(1, tp):
        z_copy(d, t).wait_send()


def fused(tp, nrows, hidden, down_weight, first, second, seg_len, seg_ad, slot_of):
    rows_each, depth = hidden.shape
    width = down_weight.shape[1]
    kc = depth // CHUNKS
    slots_each, _, rank = first.shape
    first = first.transpose(0, 2, 1)
    owned = second.shape[0] * second.shape[1]
    second = second.reshape(owned, width)
    dma = pltpu.SemaphoreType.DMA
    anywhere = pl.BlockSpec(memory_space=pl.ANY)
    scalars = pl.BlockSpec(memory_space=pltpu.SMEM)
    return pl.pallas_call(
        fused_kernel,
        out_shape=jax.ShapeDtypeStruct((rows_each, width), jnp.bfloat16),
        in_specs=[anywhere] * 4 + [scalars] * 3,
        out_specs=pl.BlockSpec(memory_space=pltpu.VMEM),
        scratch_shapes=[
            pltpu.VMEM((tp, CHUNKS, rows_each, kc), jnp.bfloat16),
            pltpu.VMEM((CHUNKS, kc, width), jnp.bfloat16),
            pltpu.VMEM((CHUNKS, slots_each, rank, kc), jnp.bfloat16),
            pltpu.VMEM((nrows, owned, width), jnp.bfloat16),
            pltpu.VMEM((tp, width // TILE, rows_each, TILE), jnp.float32),
            pltpu.VMEM((tp, rows_each, slots_each * rank), jnp.float32),
            pltpu.VMEM((tp, width // TILE, rows_each, TILE), jnp.bfloat16),
            pltpu.VMEM((2, width // TILE, rows_each, TILE), jnp.bfloat16),
            pltpu.VMEM((tp, width // TILE, rows_each, TILE), jnp.bfloat16),
            pltpu.VMEM((tp, rows_each, rank), jnp.float32),
            pltpu.VMEM((nrows, rows_each, rank), jnp.float32),
            pltpu.VMEM((rows_each, rank), jnp.float32),
            pltpu.VMEM((tp, rows_each, rank), jnp.float32),
            dma((CHUNKS,)), dma((CHUNKS,)), dma((CHUNKS,)), dma,
            dma((nrows - 1,)), dma((nrows - 1,)),
            dma((tp - 1, CHUNKS)), dma((tp - 1, CHUNKS)),
            dma((tp - 1, CHUNKS)), dma((tp - 1, CHUNKS)),
            dma((tp, width // TILE)), dma((2, width // TILE)),
            dma((tp, width // TILE)), dma((tp, width // TILE)), dma((tp,)), dma((nrows,)),
            dma((tp - 1,)), dma((tp - 1,)),
        ],
        compiler_params=pltpu.CompilerParams(
            collective_id=0, has_side_effects=True, vmem_limit_bytes=56 * 2**20
        ),
        cost_estimate=pl.CostEstimate(
            flops=2 * tp * rows_each * depth * width,
            bytes_accessed=2 * depth * width,
            transcendentals=0,
        ),
    )(hidden, down_weight, first, second, seg_len, seg_ad, slot_of)


def solution(mesh):
    placed = (
        P(("groups", "tp"), "rows"),
        P("rows", "tp"),
        P("tp", "rows", None),
        P("rows", None, "tp"),
        P("groups", None),
        P("groups", None),
        P(),
    )
    tp, nrows = mesh.shape["tp"], mesh.shape["rows"]
    body = functools.partial(fused, tp, nrows) if tp == nrows == 4 else local
    return jax.shard_map(
        body, mesh=mesh, in_specs=placed, out_specs=P(("groups", "rows"), "tp"), check_vma=False
    )
```
